32 devices in a mesh: tile: 4 (over y, x), query: 2 (over core), dp: 4 (over z).
Axes of the slice: x: 2, y: 2, z: 4, core: 2. Of those that a mesh axis runs over, the one named last changes fastest.
Arguments:
- features: bfloat16 [4, 32768, 256], P('dp', ('tile', 'query')), may hold values from -6 to 6
- queries: bfloat16 [4, 64, 256], P('dp', ('tile', 'query')), may hold values from -6 to 6
- out_grad: bfloat16 [4, 64, 256], P('dp', ('tile', 'query')), may hold values from -48 to 48
- value_weight: bfloat16 [256, 256], replicated, may hold values from -0.375 to 0.375
- attn_weight: bfloat16 [256, 128], replicated, may hold values from -0.375 to 0.375
- out_weight: bfloat16 [256, 256], replicated, may hold values from -0.375 to 0.375
- slot_point: int32 [4, 16384], P('dp', ('tile', 'query')), may hold values from 0 to 8191, as said below
- slot_rows: int32 [4, 4, 16384], P('dp', None, ('tile', 'query')), may hold values from 0 to 4095, as said below
- slot_bilinear: float32 [4, 4, 16384], P('dp', None, ('tile', 'query')), may hold values from 0 to 1, as said below
- slot_count: int32 [4, 8], P('dp', ('tile', 'query')), may hold values from 1 to 2048, as said below
Outputs:
- feature_grad: bfloat16 [4, 32768, 256], P('dp', ('tile', 'query'))
- query_grad: bfloat16 [4, 64, 256], P('dp', ('tile', 'query'))
- value_weight_grad: float32 [256, 256], replicated
- attn_weight_grad: float32 [256, 128], replicated
- out_weight_grad: float32 [256, 256], replicated
The draws below stay inside these ranges and needn't reach their ends.
Inputs may be any that keep to these rules, and one draw needn't show every extreme that they name: `slot_count`: per page one owner has exactly 2048 live slots; the counts of a page sum to 8192. `slot_point`: the live slots of a page name every sample point exactly once, point m = q * 128 + head * 4 * 4 + level * 4 + point; slots that are not live hold arbitrary point numbers. `slot_rows`: the corners of a slot are rows r, r + 1, r + 64, r + 65 of the owner's tokens laid out in lines of 64. `slot_bilinear`: the four weights of a slot sum to one.
All inputs are finite; a program needn't handle non-finite values.
Results may differ from the reference program's by a relative error of at most 0.0064.
Values may be sent and summed in bfloat16 or wider, within the bound.
A program may use at most 128 MiB of HBM per device.

```python
import jax
import jax.numpy as jnp
from jax import lax

D = 256
HEADS = 8
LEVELS = 4
POINTS = 4
TILE_W = 64
TOK_DEV = 4096
OWNERS = 8
PAGES = 4
QUERIES = 64
TOKENS = 32768
ATT = 128
CAP = 2048
SLOTS = 16384


def page_counts(page_key):
    all_points = QUERIES * HEADS * LEVELS * POINTS
    remaining = all_points - CAP
    first_key, second_key = jax.random.split(page_key)
    weights = jax.random.randint(first_key, (OWNERS,), 2, 4)
    busiest = jax.random.randint(second_key, (), 0, OWNERS)
    is_busiest = jnp.arange(OWNERS) == busiest
    weights = jnp.where(is_busiest, 0, weights)
    shares = remaining * weights // jnp.sum(weights)
    leftover = remaining - jnp.sum(shares)
    ranked = jnp.cumsum(jnp.where(is_busiest, 0, 1)) - 1
    shares = shares + jnp.where(jnp.logical_and(jnp.logical_not(is_busiest), ranked < leftover), 1, 0)
    return jnp.where(is_busiest, CAP, shares).astype(jnp.int32)


def page_points(page_key):
    all_points = QUERIES * HEADS * LEVELS * POINTS
    counts = page_counts(jax.random.fold_in(page_key, 1))
    shuffled = jax.random.permutation(jax.random.fold_in(page_key, 2), all_points).astype(jnp.int32)
    starts = jnp.cumsum(counts) - counts
    slot_ids = jnp.arange(OWNERS * CAP)
    owner_index = slot_ids // CAP
    within = slot_ids % CAP
    position = jnp.minimum(starts[owner_index] + within, all_points - 1)
    filler = jax.random.randint(jax.random.fold_in(page_key, 3), (OWNERS * CAP,), 0, all_points)
    return jnp.where(within < counts[owner_index], shuffled[position], filler).astype(jnp.int32)


def page_key_list(key):
    return jax.random.split(jax.random.fold_in(key, 5), PAGES)


def count_of_page(page_key):
    return page_counts(jax.random.fold_in(page_key, 1))


def draw_slot_count(key, part):
    return jax.vmap(count_of_page)(page_key_list(key))


def draw_slot_point(key, part):
    return jax.vmap(page_points)(page_key_list(key))


def draw_slot_rows(key, part):
    first_key, second_key = jax.random.split(jax.random.fold_in(key, 31))
    grid_lines = TOK_DEV // TILE_W
    row_y = jax.random.randint(first_key, (PAGES, SLOTS), 0, grid_lines - 1)
    row_x = jax.random.randint(second_key, (PAGES, SLOTS), 0, TILE_W - 1)
    base_row = row_y * TILE_W + row_x
    return jnp.stack([base_row, base_row + 1, base_row + TILE_W, base_row + TILE_W + 1], axis=1).astype(jnp.int32)


def draw_slot_bilinear(key, part):
    first_key, second_key = jax.random.split(jax.random.fold_in(key, 41))
    frac_x = jax.random.uniform(first_key, (PAGES, SLOTS), jnp.float32)
    frac_y = jax.random.uniform(second_key, (PAGES, SLOTS), jnp.float32)
    return jnp.stack([(1.0 - frac_x) * (1.0 - frac_y), frac_x * (1.0 - frac_y), (1.0 - frac_x) * frac_y, frac_x * frac_y], axis=1).astype(jnp.float32)


def steps_of(rng, extent, pieces, smallest, high):
    factor_of = 1.0
    for dim, shards_of in pieces:
        steps = jax.random.uniform(jax.random.fold_in(jax.random.fold_in(rng, 6), dim), (shards_of,), jnp.float32, smallest / len(pieces), high / len(pieces))
        factor_of = factor_of * jnp.repeat(jnp.exp(steps), extent[dim] // shards_of).reshape((-1,) + (1,) * (len(extent) - 1 - dim))
    return factor_of


def scatter_about(rng, shape, width, limit, pieces=(), kind=jnp.bfloat16):
    level = steps_of(rng, shape, pieces, -0.22, 0.18) if pieces else 1.0
    values = jax.random.normal(rng, shape, jnp.float32) * width * level
    return jnp.minimum(jnp.maximum(values, -limit), limit).astype(kind)


def setup_inputs(seed: int = 0) -> dict:
    keys = jax.random.split(jax.random.key(seed), 11)
    return {
        "features": scatter_about(keys[0], (PAGES, TOKENS, D), 1.0, 6.0, ((0, 4), (1, 8))),
        "queries": scatter_about(keys[1], (PAGES, QUERIES, D), 1.0, 6.0, ((0, 4), (1, 8))),
        "out_grad": scatter_about(keys[2], (PAGES, QUERIES, D), 8.0, 48.0, ((0, 4), (1, 8))),
        "value_weight": scatter_about(keys[3], (D, D), D ** -0.5, 0.375),
        "attn_weight": scatter_about(keys[4], (D, ATT), D ** -0.5, 0.375),
        "out_weight": scatter_about(keys[5], (D, D), D ** -0.5, 0.375),
        "slot_point": draw_slot_point(jax.random.fold_in(keys[10], 71), 0),
        "slot_rows": draw_slot_rows(jax.random.fold_in(keys[10], 71), 0),
        "slot_bilinear": draw_slot_bilinear(jax.random.fold_in(keys[10], 71), 0),
        "slot_count": draw_slot_count(jax.random.fold_in(keys[10], 71), 0),
    }


def over_rows(left, right):
    return lax.dot_general(left, right, (((0,), (0,)), ((), ())), preferred_element_type=jnp.float32)


def over_rows_exact(left, right):
    return lax.dot_general(left, right, (((0,), (0,)), ((), ())), precision=lax.Precision.HIGHEST, preferred_element_type=jnp.float32)


def times_transpose(left, right):
    return lax.dot_general(left, right, (((1,), (1,)), ((), ())), preferred_element_type=jnp.float32)


def reference(features, queries, out_grad, value_weight, attn_weight, out_weight, slot_point, slot_rows, slot_bilinear, slot_count):
    per_head = LEVELS * POINTS
    head_width = D // HEADS
    grad_scale = float(PAGES * QUERIES) ** -0.5

    def one_page(page_args):
        page_feats, page_queries, page_out, points, token_rows, bilinear_all, counts = page_args
        projected = jnp.dot(page_feats, value_weight, preferred_element_type=jnp.float32).astype(jnp.bfloat16)
        exponent = jnp.exp(jnp.dot(page_queries, attn_weight, preferred_element_type=jnp.float32)).reshape(QUERIES, HEADS, per_head)
        attention = (exponent / jnp.sum(exponent, axis=2, keepdims=True)).reshape(QUERIES, ATT)
        attn_rounded = attention.astype(jnp.bfloat16)
        sample_grad = times_transpose(page_out, out_weight).astype(jnp.bfloat16)
        slot_ids = jnp.arange(SLOTS, dtype=jnp.int32)
        owner_index = (slot_ids // CAP).astype(jnp.int32)
        alive_slot = (slot_ids % CAP) < counts[owner_index]
        query_index = (points // ATT).astype(jnp.int32)
        attn_column = (points % ATT).astype(jnp.int32)
        head_index = attn_column // per_head
        weight = jnp.where(alive_slot, attn_rounded[query_index, attn_column].astype(jnp.float32), jnp.zeros((), jnp.float32))
        head_mask = (jnp.arange(D, dtype=jnp.int32)[None, :] // head_width) == head_index[:, None]
        slot_grad = jnp.where(head_mask, sample_grad[query_index], jnp.zeros((), jnp.bfloat16)).astype(jnp.float32)
        mixed_rows = jnp.zeros((SLOTS, D), jnp.float32)
        corner_dots = jnp.zeros((SLOTS,), jnp.float32)
        value_grad = jnp.zeros((TOKENS, D), jnp.float32)
        for corner in range(4):
            token_row = (token_rows[corner] + owner_index * TOK_DEV).astype(jnp.int32)
            bilinear = bilinear_all[corner]
            picked = projected[token_row].astype(jnp.float32)
            mixed_rows = mixed_rows + bilinear[:, None] * picked
            corner_dots = corner_dots + bilinear * jnp.sum(picked * slot_grad, axis=1)
            value_grad = value_grad.at[token_row].add((weight * bilinear)[:, None] * slot_grad)
        sampled = jnp.zeros((QUERIES, D), jnp.float32).at[query_index].add(jnp.where(head_mask, weight[:, None] * mixed_rows, jnp.zeros((), jnp.float32)))
        attn_grad = jnp.zeros((QUERIES, ATT), jnp.float32).at[query_index, attn_column].add(jnp.where(alive_slot, corner_dots, jnp.zeros((), jnp.float32)))
        attn_three = attention.reshape(QUERIES, HEADS, per_head)
        grad_three = attn_grad.reshape(QUERIES, HEADS, per_head)
        logit_grad = (attn_three * (grad_three - jnp.sum(attn_three * grad_three, axis=2, keepdims=True))).reshape(QUERIES, ATT).astype(jnp.bfloat16)
        query_grad = times_transpose(logit_grad, attn_weight).astype(jnp.bfloat16)
        value_rounded = value_grad.astype(jnp.bfloat16)
        feature_grad = times_transpose(value_rounded, value_weight).astype(jnp.bfloat16)
        value_term = over_rows(page_feats, value_rounded)
        attn_term = over_rows(page_queries, logit_grad)
        out_term = over_rows_exact(sampled, page_out.astype(jnp.float32))
        return feature_grad, query_grad, value_term, attn_term, out_term

    results = lax.map(one_page, (features, queries, out_grad, slot_point, slot_rows, slot_bilinear, slot_count))
    feature_grad, query_grad, value_terms, attn_terms, out_terms = results
    return (feature_grad, query_grad, jnp.sum(value_terms, axis=0) * grad_scale, jnp.sum(attn_terms, axis=0) * grad_scale, jnp.sum(out_terms, axis=0) * grad_scale)
```

```python
import jax
import jax.numpy as jnp
from jax import lax
from jax.experimental import pallas as pl
from jax.experimental.pallas import tpu as pltpu
from jax.sharding import PartitionSpec as P

HEADS = 8
TILE_W = 64
MESH = pl.DeviceIdType.MESH
PAGE = ("tile", "query")


def dot(left, right, contract):
    return lax.dot_general(
        left, right, ((contract[:1], contract[1:]), ((), ())), preferred_element_type=jnp.float32
    )


def page_peer(offset):
    count = lax.axis_size(PAGE)
    cores = lax.axis_size("query")
    me = lax.axis_index("tile") * cores + lax.axis_index("query")
    peer = lax.rem(me + offset, count)
    return peer, {"tile": peer // cores, "query": lax.rem(peer, cores)}


def dp_peer(offset):
    return {"dp": lax.rem(lax.axis_index("dp") + offset, lax.axis_size("dp"))}


def greet(with_dp):
    barrier = pltpu.get_barrier_semaphore()
    count = lax.axis_size(PAGE)
    pages = lax.axis_size("dp") if with_dp else 1
    for offset in range(1, count):
        pl.semaphore_signal(barrier, inc=1, device_id=page_peer(offset)[1], device_id_type=MESH)
    for offset in range(1, pages):
        pl.semaphore_signal(barrier, inc=1, device_id=dp_peer(offset), device_id_type=MESH)
    pl.semaphore_wait(barrier, count - 1 + pages - 1)


def gather_kernel(mine_ref, every_ref, local_sem, send_sem, recv_sem):
    count = lax.axis_size(PAGE)
    me, _ = page_peer(0)
    greet(False)
    keep = pltpu.make_async_copy(mine_ref, every_ref.at[me], local_sem)
    keep.start()
    copies = []
    for offset in range(1, count):
        _, device = page_peer(offset)
        copy = pltpu.make_async_remote_copy(
            src_ref=mine_ref,
            dst_ref=every_ref.at[me],
            send_sem=send_sem.at[offset],
            recv_sem=recv_sem.at[offset],
            device_id=device,
            device_id_type=MESH,
        )
        copy.start()
        copies.append(copy)
    keep.wait()
    for copy in copies:
        copy.wait()


def page_kernel(
    count_ref,
    features_ref,
    queries_ref,
    out_grad_ref,
    value_weight_ref,
    attn_weight_ref,
    out_weight_ref,
    point_ref,
    rows_ref,
    bilinear_ref,
    feature_grad_ref,
    sums_ref,
    logit_ref,
    upper,
    lower,
    wrapped,
    corner_map,
    mixed,
    contribution,
    query_onehot,
    weight_row,
    value_total,
):
    step = pl.program_id(0)
    steps = pl.num_programs(0)
    width = value_weight_ref.shape[0]
    att_width = attn_weight_ref.shape[1]
    per_head = att_width // HEADS
    head_width = width // HEADS
    capacity = point_ref.shape[1]
    all_queries = queries_ref.shape[0]
    chunk = features_ref.shape[0]
    f32, bf16 = jnp.float32, jnp.bfloat16
    points = point_ref[...]
    column = lax.rem(points, att_width)
    head = column // per_head
    base = rows_ref[0:1, :]

    def head_mask():
        row = lax.broadcasted_iota(jnp.int32, (width, capacity), 0)
        return row // head_width == head

    def grad_rows():
        sample_grad = dot(out_weight_ref[...], out_grad_ref[...], (1, 1)).astype(bf16)
        return dot(sample_grad, query_onehot[...], (1, 0))

    def attention_of():
        exponent = jnp.exp(dot(queries_ref[...], attn_weight_ref[...], (1, 0)))
        return exponent / head_sum(exponent)

    def head_sum(values):
        same = (
            lax.broadcasted_iota(jnp.int32, (att_width, att_width), 0) // per_head
            == lax.broadcasted_iota(jnp.int32, (att_width, att_width), 1) // per_head
        )
        return lax.dot_general(
            values,
            jnp.where(same, 1.0, 0.0).astype(f32),
            (((1,), (0,)), ((), ())),
            precision=lax.Precision.HIGHEST,
            preferred_element_type=f32,
        )

    @pl.when(step == 0)
    def _():
        x = lax.rem(base, TILE_W)
        lane = lax.broadcasted_iota(jnp.int32, (TILE_W, capacity), 0)
        here, beside = lane == x, lane == x + 1
        over = jnp.logical_and(x == TILE_W - 1, lane == 0)
        b0, b1 = bilinear_ref[0:1, :], bilinear_ref[1:2, :]
        b2, b3 = bilinear_ref[2:3, :], bilinear_ref[3:4, :]
        zero = jnp.zeros((), f32)
        upper[...] = (jnp.where(here, b0, zero) + jnp.where(beside, b1, zero)).astype(bf16)
        lower[...] = (
            jnp.where(here, b2, zero) + jnp.where(beside, b3, zero) + jnp.where(over, b1, zero)
        ).astype(bf16)
        wrapped[...] = jnp.where(over, b3, zero)[0:16].astype(bf16)
        which = lax.broadcasted_iota(jnp.int32, (all_queries, capacity), 0)
        query_onehot[...] = jnp.where(which == points // att_width, 1.0, 0.0).astype(bf16)
        attn_rows = dot(attention_of().astype(bf16), query_onehot[...], (0, 0))
        attn_lane = lax.broadcasted_iota(jnp.int32, (att_width, capacity), 0)
        picked = jnp.sum(jnp.where(attn_lane == column, attn_rows, zero), axis=0, keepdims=True)
        slot = lax.broadcasted_iota(jnp.int32, (1, capacity), 1)
        weight = jnp.where(slot < count_ref[0, 0], picked, zero)
        weight_row[...] = weight
        spread = jnp.where(head_mask(), grad_rows() * weight, zero)
        contribution[...] = spread.T.astype(bf16)

    line = base // TILE_W
    for index in range(chunk // TILE_W):
        here = line - (step * (chunk // TILE_W) + index)

        def mask(shift):
            one = jnp.where(here == -shift, 1.0, 0.0).astype(f32)
            return jnp.broadcast_to(one, (16, capacity)).astype(bf16)

        first, second, third = mask(0), mask(1), mask(2)
        for part in range(TILE_W // 16):
            rows = slice(part * 16, part * 16 + 16)
            block = upper[rows] * first + lower[rows] * second
            if part == 0:
                block = block + wrapped[...] * third
            corner_map[index * TILE_W + part * 16 : index * TILE_W + part * 16 + 16, :] = block

    projected = dot(value_weight_ref[...], features_ref[...], (0, 1)).astype(bf16)
    added = dot(projected, corner_map[...], (1, 0))

    @pl.when(step == 0)
    def _():
        mixed[...] = added

    @pl.when(step > 0)
    def _():
        mixed[...] += added

    value_rounded = dot(corner_map[...], contribution[...], (1, 0)).astype(bf16)
    feature_grad_ref[...] = dot(value_rounded, value_weight_ref[...], (1, 1)).astype(bf16)
    term = dot(features_ref[...], value_rounded, (0, 0))

    @pl.when(step == 0)
    def _():
        value_total[...] = term

    @pl.when(step > 0)
    def _():
        value_total[...] += term

    @pl.when(step == steps - 1)
    def _():
        zero = jnp.zeros((), f32)
        own = jnp.where(head_mask(), mixed[...], zero)
        dots = jnp.sum(own * grad_rows(), axis=0, keepdims=True)
        slot = lax.broadcasted_iota(jnp.int32, (1, capacity), 1)
        dots = jnp.where(slot < count_ref[0, 0], dots, zero)
        attn_lane = lax.broadcasted_iota(jnp.int32, (att_width, capacity), 0)
        table = jnp.where(attn_lane == column, dots, zero)
        high = table.astype(bf16)
        low = (table - high.astype(f32)).astype(bf16)
        attn_grad = dot(query_onehot[...], high, (1, 1)) + dot(query_onehot[...], low, (1, 1))
        attention = attention_of()
        logit = attention * (attn_grad - head_sum(attention * attn_grad))
        logit_ref[...] = logit
        sampled = dot((own * weight_row[...]).astype(bf16), query_onehot[...], (1, 1))
        sampled_high = sampled.astype(bf16)
        sampled_low = (sampled - sampled_high.astype(f32)).astype(bf16)
        out_grad = out_grad_ref[...]
        kind = sums_ref.dtype
        sums_ref[:, 0:width] = value_total[...].astype(kind)
        sums_ref[:, width : 2 * width] = (
            dot(sampled_high, out_grad, (1, 0)) + dot(sampled_low, out_grad, (1, 0))
        ).astype(kind)
        sums_ref[:, 2 * width :] = dot(queries_ref[...], logit.astype(bf16), (0, 0)).astype(kind)


def sum_kernel(
    sums_ref,
    logit_ref,
    attn_weight_ref,
    total_ref,
    query_grad_ref,
    from_page,
    from_dp,
    from_logit,
    page_send,
    page_recv,
    logit_send,
    logit_recv,
    dp_send,
    dp_recv,
    all_send,
    all_recv,
):
    count = lax.axis_size(PAGE)
    pages = lax.axis_size("dp")
    me, _ = page_peer(0)
    f32 = jnp.float32
    kind = sums_ref.dtype
    greet(True)

    def remote(source, target, send, recv, offset, device):
        copy = pltpu.make_async_remote_copy(
            src_ref=source,
            dst_ref=target,
            send_sem=send.at[offset],
            recv_sem=recv.at[offset],
            device_id=device,
            device_id_type=MESH,
        )
        copy.start()
        return copy

    page_copies, logit_copies = [], []
    for offset in range(1, count):
        peer, device = page_peer(offset)
        page_copies.append(
            remote(sums_ref.at[peer], from_page.at[offset], page_send, page_recv, offset, device)
        )
    for offset in range(1, count):
        peer, device = page_peer(offset)
        logit_copies.append(
            remote(
                logit_ref.at[peer], from_logit.at[offset], logit_send, logit_recv, offset, device
            )
        )
    total = sums_ref[me].astype(f32)
    for offset in range(1, count):
        page_copies[offset - 1].wait()
        total = total + from_page[offset].astype(f32)
    from_dp[0] = total.astype(kind)
    dp_copies = []
    for offset in range(1, pages):
        dp_copies.append(
            remote(from_dp.at[0], from_dp.at[offset], dp_send, dp_recv, offset, dp_peer(offset))
        )
    logit = logit_ref[me]
    for offset in range(1, count):
        logit_copies[offset - 1].wait()
        logit = logit + from_logit[offset]
    query_grad_ref[...] = dot(
        logit.astype(jnp.bfloat16), attn_weight_ref[...], (1, 1)
    ).astype(jnp.bfloat16)
    for offset in range(1, pages):
        dp_copies[offset - 1].wait()
    total = from_dp[0].astype(f32)
    if pages > 1:
        mine = lax.axis_index("dp")
        total = jnp.zeros_like(total)
        for page in range(pages):
            total = total + from_dp[lax.rem(mine + pages - page, pages)].astype(f32)
    total_ref[me] = total.astype(kind)
    all_copies = []
    for offset in range(1, count):
        _, device = page_peer(offset)
        all_copies.append(
            remote(total_ref.at[me], total_ref.at[me], all_send, all_recv, offset, device)
        )
    for copy in all_copies:
        copy.wait()


def whole(shape):
    return pl.BlockSpec(shape, lambda step: (0,) * len(shape))


def local(
    features,
    queries,
    out_grad,
    value_weight,
    attn_weight,
    out_weight,
    slot_point,
    slot_rows,
    slot_bilinear,
    slot_count,
):
    owners = lax.axis_size(PAGE)
    page_count = lax.axis_size("dp")
    local_queries = queries.shape[1]
    all_queries = local_queries * owners
    grad_scale = float(page_count * all_queries) ** (-0.5)
    tokens, width = features.shape[1:]
    att_width = attn_weight.shape[1]
    capacity = slot_point.shape[1]
    f32, bf16 = jnp.float32, jnp.bfloat16
    vmem = pl.BlockSpec(memory_space=pltpu.VMEM)
    dma = pltpu.SemaphoreType.DMA

    every = pl.pallas_call(
        gather_kernel,
        out_shape=jax.ShapeDtypeStruct((owners, 2 * local_queries, width), bf16),
        in_specs=[vmem],
        out_specs=vmem,
        scratch_shapes=[dma, dma((owners,)), dma((owners,))],
        compiler_params=pltpu.CompilerParams(collective_id=0, has_side_effects=True),
    )(jnp.concatenate([queries[0], out_grad[0]], axis=0))
    every_query = every[:, :local_queries].reshape(all_queries, width)
    every_out = every[:, local_queries:].reshape(all_queries, width)

    sum_width = 2 * width + att_width
    sum_rows = width // owners
    kind = bf16 if sum_rows % 16 == 0 else f32
    chunk = 512
    feature_grad, sums, logit = pl.pallas_call(
        page_kernel,
        grid=(tokens // chunk,),
        out_shape=(
            jax.ShapeDtypeStruct((tokens, width), bf16),
            jax.ShapeDtypeStruct((width, sum_width), kind),
            jax.ShapeDtypeStruct((all_queries, att_width), f32),
        ),
        in_specs=[
            pl.BlockSpec(memory_space=pltpu.SMEM),
            pl.BlockSpec((chunk, width), lambda step: (step, 0)),
            whole((all_queries, width)),
            whole((all_queries, width)),
            whole((width, width)),
            whole((width, att_width)),
            whole((width, width)),
            whole((1, capacity)),
            whole((4, capacity)),
            whole((4, capacity)),
        ],
        out_specs=(
            pl.BlockSpec((chunk, width), lambda step: (step, 0)),
            whole((width, sum_width)),
            whole((all_queries, att_width)),
        ),
        scratch_shapes=[
            pltpu.VMEM((TILE_W, capacity), bf16),
            pltpu.VMEM((TILE_W, capacity), bf16),
            pltpu.VMEM((16, capacity), bf16),
            pltpu.VMEM((chunk, capacity), bf16),
            pltpu.VMEM((width, capacity), f32),
            pltpu.VMEM((capacity, width), bf16),
            pltpu.VMEM((all_queries, capacity), bf16),
            pltpu.VMEM((1, capacity), f32),
            pltpu.VMEM((width, width), f32),
        ],
        compiler_params=pltpu.CompilerParams(vmem_limit_bytes=48 * 1024 * 1024),
    )(
        slot_count,
        features[0],
        every_query,
        every_out,
        value_weight,
        attn_weight,
        out_weight,
        slot_point,
        slot_rows[0],
        slot_bilinear[0],
    )

    total, query_grad = pl.pallas_call(
        sum_kernel,
        out_shape=(
            jax.ShapeDtypeStruct((owners, sum_rows, sum_width), kind),
            jax.ShapeDtypeStruct((local_queries, width), bf16),
        ),
        in_specs=[vmem] * 3,
        out_specs=(vmem, vmem),
        scratch_shapes=[
            pltpu.VMEM((owners, sum_rows, sum_width), kind),
            pltpu.VMEM((page_count, sum_rows, sum_width), kind),
            pltpu.VMEM((owners, local_queries, att_width), f32),
            dma((owners,)),
            dma((owners,)),
            dma((owners,)),
            dma((owners,)),
            dma((page_count,)),
            dma((page_count,)),
            dma((owners,)),
            dma((owners,)),
        ],
        compiler_params=pltpu.CompilerParams(
            collective_id=1, has_side_effects=True, vmem_limit_bytes=32 * 1024 * 1024
        ),
    )(
        sums.reshape(owners, sum_rows, sum_width),
        logit.reshape(owners, local_queries, att_width),
        attn_weight,
    )
    total = total.reshape(width, sum_width)
    return (
        feature_grad[None],
        query_grad[None],
        total[:, :width].astype(f32) * grad_scale,
        total[:, 2 * width :].astype(f32) * grad_scale,
        total[:, width : 2 * width].astype(f32) * grad_scale,
    )


def solution(mesh):
    in_specs = (
        P("dp", ("tile", "query"), None),
        P("dp", ("tile", "query"), None),
        P("dp", ("tile", "query"), None),
        P(),
        P(),
        P(),
        P("dp", ("tile", "query")),
        P("dp", None, ("tile", "query")),
        P("dp", None, ("tile", "query")),
        P("dp", ("tile", "query")),
    )
    out_specs = (P("dp", ("tile", "query"), None), P("dp", ("tile", "query"), None), P(), P(), P())
    return jax.shard_map(local, mesh=mesh, in_specs=in_specs, out_specs=out_specs, check_vma=False)
```

```python
import jax
import jax.numpy as jnp
from jax import lax
from jax.experimental import pallas as pl
from jax.experimental.pallas import tpu as pltpu
from jax.sharding import PartitionSpec as P

HEADS = 8
TILE_W = 64
MESH = pl.DeviceIdType.MESH
PAGE = ("tile", "query")
CHUNK = 512


def dot(left, right, contract):
    return lax.dot_general(
        left, right, ((contract[:1], contract[1:]), ((), ())), preferred_element_type=jnp.float32
    )


def page_peer(offset):
    count = lax.axis_size(PAGE)
    cores = lax.axis_size("query")
    me = lax.axis_index("tile") * cores + lax.axis_index("query")
    peer = lax.rem(me + offset, count)
    return peer, {"tile": peer // cores, "query": lax.rem(peer, cores)}


def dp_peer(offset):
    return {"dp": lax.rem(lax.axis_index("dp") + offset, lax.axis_size("dp"))}


def greet():
    barrier = pltpu.get_barrier_semaphore()
    count = lax.axis_size(PAGE)
    pages = lax.axis_size("dp")
    for offset in range(1, count):
        pl.semaphore_signal(barrier, inc=1, device_id=page_peer(offset)[1], device_id_type=MESH)
    for offset in range(1, pages):
        pl.semaphore_signal(barrier, inc=1, device_id=dp_peer(offset), device_id_type=MESH)
    pl.semaphore_wait(barrier, count - 1 + pages - 1)


def remote(source, target, sems, offset, device):
    copy = pltpu.make_async_remote_copy(
        src_ref=source,
        dst_ref=target,
        send_sem=sems.at[0, offset],
        recv_sem=sems.at[1, offset],
        device_id=device,
        device_id_type=MESH,
    )
    copy.start()
    return copy


class Exchange:
    def __init__(self, mine, from_page, from_dp, total, page_sems, dp_sems, all_sems):
        self.mine, self.from_page, self.from_dp, self.total = mine, from_page, from_dp, total
        self.page_sems, self.dp_sems, self.all_sems = page_sems, dp_sems, all_sems
        self.count, self.pages = lax.axis_size(PAGE), lax.axis_size("dp")

    def send_page(self):
        self.copies = []
        for offset in range(1, self.count):
            peer, device = page_peer(offset)
            target = self.from_page.at[offset]
            self.copies.append(
                remote(self.mine.at[peer], target, self.page_sems, offset, device)
            )

    def send_dp(self):
        me, _ = page_peer(0)
        total = self.mine[me].astype(jnp.float32)
        for offset in range(1, self.count):
            self.copies[offset - 1].wait()
            total = total + self.from_page[offset].astype(jnp.float32)
        self.from_dp[0] = total.astype(self.from_dp.dtype)
        self.copies = []
        for offset in range(1, self.pages):
            target = self.from_dp.at[offset]
            self.copies.append(
                remote(self.from_dp.at[0], target, self.dp_sems, offset, dp_peer(offset))
            )

    def send_all(self):
        me, _ = page_peer(0)
        for copy in self.copies:
            copy.wait()
        mine = lax.axis_index("dp")
        total = jnp.zeros(self.mine.shape[1:], jnp.float32)
        for page in range(self.pages):
            source = lax.rem(mine + self.pages - page, self.pages)
            total = total + self.from_dp[source].astype(jnp.float32)
        self.total[me] = total.astype(self.total.dtype)
        self.copies = []
        for offset in range(1, self.count):
            _, device = page_peer(offset)
            self.copies.append(
                remote(self.total.at[me], self.total.at[me], self.all_sems, offset, device)
            )

    def finish(self):
        for copy in self.copies:
            copy.wait()


def page_kernel(
    count_ref,
    features_hbm,
    query_ref,
    grad_ref,
    value_weight_ref,
    attn_weight_ref,
    out_weight_ref,
    point_ref,
    rows_ref,
    bilinear_ref,
    feature_grad_hbm,
    query_grad_ref,
    early_total,
    late_total,
    features,
    feature_grad,
    packed,
    every,
    upper,
    lower,
    wrapped,
    corner_map,
    mixed,
    grad_rows,
    contribution,
    query_onehot,
    value_total,
    early,
    early_page,
    early_dp,
    late,
    late_page,
    late_dp,
    logit_parts,
    from_logit,
    local_sem,
    in_sems,
    out_sems,
    gather_sems,
    logit_sems,
    early_page_sems,
    early_dp_sems,
    early_all_sems,
    late_page_sems,
    late_dp_sems,
    late_all_sems,
):
    f32, bf16 = jnp.float32, jnp.bfloat16
    owners = lax.axis_size(PAGE)
    me, _ = page_peer(0)
    width = value_weight_ref.shape[0]
    att_width = attn_weight_ref.shape[1]
    per_head = att_width // HEADS
    head_width = width // HEADS
    capacity = point_ref.shape[1]
    local_queries = query_ref.shape[0]
    all_queries = local_queries * owners
    tokens = features.shape[0]
    chunk = CHUNK
    steps = tokens // chunk
    zero = jnp.zeros((), f32)

    def rows_of(index):
        return pl.ds(pl.multiple_of(index * chunk, chunk), chunk)

    def copy_in(index):
        rows = rows_of(index)
        return pltpu.make_async_copy(features_hbm.at[rows], features.at[rows], in_sems.at[index])

    def copy_out(index):
        rows = rows_of(index)
        return pltpu.make_async_copy(
            feature_grad.at[rows], feature_grad_hbm.at[rows], out_sems.at[index]
        )

    @pl.loop(0, steps)
    def _(index):
        copy_in(index).start()

    packed[...] = jnp.concatenate(
        [query_ref[...].astype(f32), grad_ref[...].astype(f32)], axis=0
    ).astype(bf16)
    greet()
    keep = pltpu.make_async_copy(packed, every.at[me], local_sem)
    keep.start()
    gathers = []
    for offset in range(1, owners):
        _, device = page_peer(offset)
        gathers.append(remote(packed, every.at[me], gather_sems, offset, device))

    points = point_ref[...]
    column = lax.rem(points, att_width)
    head = lax.div(column, per_head)
    base = rows_ref[0:1, :]
    x = lax.rem(base, TILE_W)
    lane = lax.broadcasted_iota(jnp.int32, (TILE_W, capacity), 0)
    here, beside = lane == x, lane == x + 1
    over = jnp.logical_and(x == TILE_W - 1, lane == 0)
    b0, b1 = bilinear_ref[0:1, :], bilinear_ref[1:2, :]
    b2, b3 = bilinear_ref[2:3, :], bilinear_ref[3:4, :]
    upper[...] = (jnp.where(here, b0, zero) + jnp.where(beside, b1, zero)).astype(bf16)
    lower[...] = (
        jnp.where(here, b2, zero) + jnp.where(beside, b3, zero) + jnp.where(over, b1, zero)
    ).astype(bf16)
    wrapped[...] = jnp.where(over, b3, zero)[0:16].astype(bf16)
    which = lax.broadcasted_iota(jnp.int32, (all_queries, capacity), 0)
    query_onehot[...] = jnp.where(which == lax.div(points, att_width), 1.0, 0.0).astype(bf16)
    mixed[...] = jnp.zeros_like(mixed)
    line = lax.div(base, TILE_W)

    @pl.loop(0, steps)
    def _(step):
        for index in range(chunk // TILE_W):
            ahead = line - (step * (chunk // TILE_W) + index)

            def mask(shift):
                one = jnp.where(ahead == -shift, 1.0, 0.0).astype(f32)
                return jnp.broadcast_to(one, (16, capacity)).astype(bf16)

            first, second, third = mask(0), mask(1), mask(2)
            for part in range(TILE_W // 16):
                rows = slice(part * 16, part * 16 + 16)
                block = upper[rows] * first + lower[rows] * second
                if part == 0:
                    block = block + wrapped[...] * third
                place = pl.multiple_of(step * chunk + index * TILE_W + part * 16, 16)
                corner_map[pl.ds(place, 16), :] = block
        copy_in(step).wait()
        rows = rows_of(step)
        projected = dot(value_weight_ref[...], features[rows], (0, 1)).astype(bf16)
        mixed[...] += dot(projected, corner_map[rows], (1, 0))

    keep.wait()
    for copy in gathers:
        copy.wait()
    everything = every[...].astype(f32)
    queries = everything[:, :local_queries].reshape(all_queries, width).astype(bf16)
    out_grad = everything[:, local_queries:].reshape(all_queries, width).astype(bf16)

    def head_sum(values):
        same = lax.div(
            lax.broadcasted_iota(jnp.int32, (att_width, att_width), 0), per_head
        ) == lax.div(lax.broadcasted_iota(jnp.int32, (att_width, att_width), 1), per_head)
        return lax.dot_general(
            values,
            jnp.where(same, 1.0, 0.0).astype(f32),
            (((1,), (0,)), ((), ())),
            precision=lax.Precision.HIGHEST,
            preferred_element_type=f32,
        )

    exponent = jnp.exp(dot(queries, attn_weight_ref[...], (1, 0)))
    attention = exponent / head_sum(exponent)
    attn_rows = dot(attention.astype(bf16), query_onehot[...], (0, 0))
    attn_lane = lax.broadcasted_iota(jnp.int32, (att_width, capacity), 0)
    picked = jnp.sum(jnp.where(attn_lane == column, attn_rows, zero), axis=0, keepdims=True)
    alive = lax.broadcasted_iota(jnp.int32, (1, capacity), 1) < count_ref[0, 0]
    weight = jnp.where(alive, picked, zero)
    sample_grad = dot(out_weight_ref[...], out_grad, (1, 1)).astype(bf16)
    grad_rows[...] = dot(sample_grad, query_onehot[...], (1, 0))
    dots = jnp.zeros((1, capacity), f32)
    for index in range(HEADS):
        rows = slice(index * head_width, (index + 1) * head_width)
        match = head == index
        block, pulled = grad_rows[rows], mixed[rows]
        dots = dots + jnp.where(match, jnp.sum(block * pulled, axis=0, keepdims=True), zero)
        scaled = jnp.where(match, weight, zero)
        contribution[:, rows] = (block * scaled).astype(bf16).T
        mixed[rows] = pulled * scaled
    dots = jnp.where(alive, dots, zero)
    table = jnp.where(attn_lane == column, dots, zero)
    high = table.astype(bf16)
    low = (table - high.astype(f32)).astype(bf16)
    attn_grad = dot(query_onehot[...], high, (1, 1)) + dot(query_onehot[...], low, (1, 1))
    logit = attention * (attn_grad - head_sum(attention * attn_grad))
    logit_parts[...] = logit.reshape(logit_parts.shape)
    logit_copies = []
    for offset in range(1, owners):
        peer, device = page_peer(offset)
        logit_copies.append(
            remote(logit_parts.at[peer], from_logit.at[offset], logit_sems, offset, device)
        )
    sampled = dot(mixed[...].astype(bf16), query_onehot[...], (1, 1))
    sampled_high = sampled.astype(bf16)
    sampled_low = (sampled - sampled_high.astype(f32)).astype(bf16)
    out_term = dot(sampled_high, out_grad, (1, 0)) + dot(sampled_low, out_grad, (1, 0))
    attn_term = dot(queries, logit.astype(bf16), (0, 0))
    kind = early.dtype
    per_owner = early.shape[:2]
    early[:, :, :width] = out_term.reshape(per_owner + (width,)).astype(kind)
    early[:, :, width:] = attn_term.reshape(per_owner + (att_width,)).astype(kind)
    early_sum = Exchange(
        early, early_page, early_dp, early_total, early_page_sems, early_dp_sems, early_all_sems
    )
    late_sum = Exchange(
        late, late_page, late_dp, late_total, late_page_sems, late_dp_sems, late_all_sems
    )
    early_sum.send_page()
    value_total[...] = jnp.zeros_like(value_total)

    def value_steps(first, last):
        @pl.loop(first, last)
        def _(step):
            rows = rows_of(step)
            value_rounded = dot(corner_map[rows], contribution[...], (1, 0)).astype(bf16)
            value_total[...] += dot(features[rows], value_rounded, (0, 0))
            feature_grad[rows] = dot(value_rounded, value_weight_ref[...], (1, 1)).astype(bf16)
            copy_out(step).start()

    value_steps(0, steps // 2)
    early_sum.send_dp()
    value_steps(steps // 2, steps)
    late[...] = value_total[...].reshape(late.shape).astype(kind)
    late_sum.send_page()
    early_sum.send_all()
    total = logit_parts[me]
    for offset in range(1, owners):
        logit_copies[offset - 1].wait()
        total = total + from_logit[offset]
    query_grad_ref[...] = dot(total.astype(bf16), attn_weight_ref[...], (1, 1)).astype(bf16)
    late_sum.send_dp()
    early_sum.finish()
    late_sum.send_all()

    @pl.loop(0, steps)
    def _(index):
        copy_out(index).wait()

    late_sum.finish()


def local(
    features,
    queries,
    out_grad,
    value_weight,
    attn_weight,
    out_weight,
    slot_point,
    slot_rows,
    slot_bilinear,
    slot_count,
):
    owners = lax.axis_size(PAGE)
    page_count = lax.axis_size("dp")
    local_queries = queries.shape[1]
    all_queries = local_queries * owners
    grad_scale = float(page_count * all_queries) ** (-0.5)
    tokens, width = features.shape[1:]
    att_width = attn_weight.shape[1]
    capacity = slot_point.shape[1]
    f32, bf16 = jnp.float32, jnp.bfloat16
    vmem = pl.BlockSpec(memory_space=pltpu.VMEM)
    dma = pltpu.SemaphoreType.DMA

    any_space = pl.BlockSpec(memory_space=pl.ANY)
    rows = width // owners
    kind = bf16 if rows % 16 == 0 else f32
    early_width = width + att_width
    steps = tokens // CHUNK
    feature_grad, query_grad, early, late = pl.pallas_call(
        page_kernel,
        out_shape=(
            jax.ShapeDtypeStruct((tokens, width), bf16),
            jax.ShapeDtypeStruct((local_queries, width), bf16),
            jax.ShapeDtypeStruct((owners, rows, early_width), kind),
            jax.ShapeDtypeStruct((owners, rows, width), kind),
        ),
        in_specs=[pl.BlockSpec(memory_space=pltpu.SMEM), any_space] + [vmem] * 8,
        out_specs=(any_space, vmem, vmem, vmem),
        scratch_shapes=[
            pltpu.VMEM((tokens, width), bf16),
            pltpu.VMEM((tokens, width), bf16),
            pltpu.VMEM((2 * local_queries, width), bf16),
            pltpu.VMEM((owners, 2 * local_queries, width), bf16),
            pltpu.VMEM((TILE_W, capacity), bf16),
            pltpu.VMEM((TILE_W, capacity), bf16),
            pltpu.VMEM((16, capacity), bf16),
            pltpu.VMEM((tokens, capacity), bf16),
            pltpu.VMEM((width, capacity), f32),
            pltpu.VMEM((width, capacity), f32),
            pltpu.VMEM((capacity, width), bf16),
            pltpu.VMEM((all_queries, capacity), bf16),
            pltpu.VMEM((width, width), f32),
            pltpu.VMEM((owners, rows, early_width), kind),
            pltpu.VMEM((owners, rows, early_width), kind),
            pltpu.VMEM((page_count, rows, early_width), kind),
            pltpu.VMEM((owners, rows, width), kind),
            pltpu.VMEM((owners, rows, width), kind),
            pltpu.VMEM((page_count, rows, width), kind),
            pltpu.VMEM((owners, local_queries, att_width), f32),
            pltpu.VMEM((owners, local_queries, att_width), f32),
            dma,
            dma((steps,)),
            dma((steps,)),
            dma((2, owners)),
            dma((2, owners)),
            dma((2, owners)),
            dma((2, page_count)),
            dma((2, owners)),
            dma((2, owners)),
            dma((2, page_count)),
            dma((2, owners)),
        ],
        compiler_params=pltpu.CompilerParams(
            collective_id=0, has_side_effects=True, vmem_limit_bytes=60 * 1024 * 1024
        ),
    )(
        slot_count,
        features[0],
        queries[0],
        out_grad[0],
        value_weight,
        attn_weight,
        out_weight,
        slot_point,
        slot_rows[0],
        slot_bilinear[0],
    )
    early = early.reshape(width, early_width)
    late = late.reshape(width, width)
    return (
        feature_grad[None],
        query_grad[None],
        late.astype(f32) * grad_scale,
        early[:, width:].astype(f32) * grad_scale,
        early[:, :width].astype(f32) * grad_scale,
    )


def solution(mesh):
    in_specs = (
        P("dp", ("tile", "query"), None),
        P("dp", ("tile", "query"), None),
        P("dp", ("tile", "query"), None),
        P(),
        P(),
        P(),
        P("dp", ("tile", "query")),
        P("dp", None, ("tile", "query")),
        P("dp", None, ("tile", "query")),
        P("dp", ("tile", "query")),
    )
    out_specs = (P("dp", ("tile", "query"), None), P("dp", ("tile", "query"), None), P(), P(), P())
    return jax.shard_map(local, mesh=mesh, in_specs=in_specs, out_specs=out_specs, check_vma=False)
```

```python
import jax
import jax.numpy as jnp
from jax import lax
from jax.experimental import pallas as pl
from jax.experimental.pallas import tpu as pltpu
from jax.sharding import PartitionSpec as P

HEADS = 8
TILE_W = 64
MESH = pl.DeviceIdType.MESH
PAGE = ("tile", "query")
CHUNK = 1024


def dot(left, right, contract):
    return lax.dot_general(
        left, right, ((contract[:1], contract[1:]), ((), ())), preferred_element_type=jnp.float32
    )


def page_peer(offset):
    count = lax.axis_size(PAGE)
    cores = lax.axis_size("query")
    me = lax.axis_index("tile") * cores + lax.axis_index("query")
    peer = lax.rem(me + offset, count)
    return peer, {"tile": peer // cores, "query": lax.rem(peer, cores)}


def dp_peer(offset):
    return {"dp": lax.rem(lax.axis_index("dp") + offset, lax.axis_size("dp"))}


def greet_all():
    barrier = pltpu.get_barrier_semaphore()
    count = lax.axis_size(PAGE)
    pages = lax.axis_size("dp")
    for offset in range(1, count):
        pl.semaphore_signal(barrier, inc=1, device_id=page_peer(offset)[1], device_id_type=MESH)
    for offset in range(1, pages):
        pl.semaphore_signal(barrier, inc=1, device_id=dp_peer(offset), device_id_type=MESH)


def await_all():
    barrier = pltpu.get_barrier_semaphore()
    pl.semaphore_wait(barrier, lax.axis_size(PAGE) + lax.axis_size("dp") - 2)


def remote(source, target, sems, offset, device):
    copy = pltpu.make_async_remote_copy(
        src_ref=source,
        dst_ref=target,
        send_sem=sems.at[0, offset],
        recv_sem=sems.at[1, offset],
        device_id=device,
        device_id_type=MESH,
    )
    copy.start()
    return copy


class Exchange:
    def __init__(self, mine, from_page, from_dp, total, page_sems, dp_sems, all_sems):
        self.mine, self.from_page, self.from_dp, self.total = mine, from_page, from_dp, total
        self.page_sems, self.dp_sems, self.all_sems = page_sems, dp_sems, all_sems
        self.count, self.pages = lax.axis_size(PAGE), lax.axis_size("dp")

    def send_page(self):
        self.copies = []
        for offset in range(1, self.count):
            peer, device = page_peer(offset)
            target = self.from_page.at[offset]
            self.copies.append(
                remote(self.mine.at[peer], target, self.page_sems, offset, device)
            )

    def send_dp(self):
        me, _ = page_peer(0)
        total = self.mine[me].astype(jnp.float32)
        for offset in range(1, self.count):
            self.copies[offset - 1].wait()
            total = total + self.from_page[offset].astype(jnp.float32)
        self.from_dp[0] = total.astype(self.from_dp.dtype)
        self.copies = []
        for offset in range(1, self.pages):
            target = self.from_dp.at[offset]
            self.copies.append(
                remote(self.from_dp.at[0], target, self.dp_sems, offset, dp_peer(offset))
            )

    def send_all(self):
        me, _ = page_peer(0)
        for copy in self.copies:
            copy.wait()
        mine = lax.axis_index("dp")
        total = jnp.zeros(self.mine.shape[1:], jnp.float32)
        for page in range(self.pages):
            source = lax.rem(mine + self.pages - page, self.pages)
            total = total + self.from_dp[source].astype(jnp.float32)
        self.total[me] = total.astype(self.total.dtype)
        self.copies = []
        for offset in range(1, self.count):
            _, device = page_peer(offset)
            self.copies.append(
                remote(self.total.at[me], self.total.at[me], self.all_sems, offset, device)
            )

    def finish(self):
        for copy in self.copies:
            copy.wait()


def page_kernel(
    count_ref,
    features_hbm,
    query_ref,
    grad_ref,
    value_weight_ref,
    attn_weight_ref,
    out_weight_ref,
    point_ref,
    rows_ref,
    bilinear_ref,
    value_grad_hbm,
    query_grad_ref,
    value_weight_grad,
    out_weight_grad,
    attn_weight_grad,
    early_total,
    late_total,
    line_rows,
    features,
    value_grad,
    packed,
    every,
    upper,
    lower,
    wrapped,
    corner_map,
    mixed,
    grad_rows,
    contribution,
    query_onehot,
    value_total,
    early,
    early_page,
    early_dp,
    late,
    late_page,
    late_dp,
    logit_parts,
    from_logit,
    local_sem,
    in_sems,
    out_sems,
    gather_sems,
    logit_sems,
    early_page_sems,
    early_dp_sems,
    early_all_sems,
    late_page_sems,
    late_dp_sems,
    late_all_sems,
):
    f32, bf16 = jnp.float32, jnp.bfloat16
    owners = lax.axis_size(PAGE)
    me, _ = page_peer(0)
    width = value_weight_ref.shape[0]
    att_width = attn_weight_ref.shape[1]
    per_head = att_width // HEADS
    head_width = width // HEADS
    capacity = point_ref.shape[1]
    local_queries = query_ref.shape[0]
    all_queries = local_queries * owners
    tokens = features.shape[0]
    chunk = CHUNK
    steps = tokens // chunk
    zero = jnp.zeros((), f32)

    def rows_of(index):
        return pl.ds(pl.multiple_of(index * chunk, chunk), chunk)

    def copy_in(index):
        rows = rows_of(index)
        return pltpu.make_async_copy(features_hbm.at[rows], features.at[rows], in_sems.at[index])

    def copy_out(index):
        rows = rows_of(index)
        return pltpu.make_async_copy(
            value_grad.at[rows], value_grad_hbm.at[rows], out_sems.at[index]
        )

    @pl.loop(0, steps)
    def _(index):
        copy_in(index).start()

    greet_all()
    points = point_ref[...]
    column = lax.rem(points, att_width)
    head = lax.div(column, per_head)
    base = rows_ref[0:1, :]
    x = lax.rem(base, TILE_W)
    lane = lax.broadcasted_iota(jnp.int32, (TILE_W, capacity), 0)
    here, beside = lane == x, lane == x + 1
    over = jnp.logical_and(x == TILE_W - 1, lane == 0)
    b0, b1 = bilinear_ref[0:1, :], bilinear_ref[1:2, :]
    b2, b3 = bilinear_ref[2:3, :], bilinear_ref[3:4, :]
    upper[...] = (jnp.where(here, b0, zero) + jnp.where(beside, b1, zero)).astype(bf16)
    lower[...] = (
        jnp.where(here, b2, zero) + jnp.where(beside, b3, zero) + jnp.where(over, b1, zero)
    ).astype(bf16)
    wrapped[...] = jnp.where(over, b3, zero)[0:16].astype(bf16)
    which = lax.broadcasted_iota(jnp.int32, (all_queries, capacity), 0)
    query_onehot[...] = jnp.where(which == lax.div(points, att_width), 1.0, 0.0).astype(bf16)
    mixed[...] = jnp.zeros_like(mixed)
    line = lax.div(base, TILE_W)

    line_rows[...] = jnp.broadcast_to(line.astype(f32), (16, capacity)).astype(bf16)

    def sample_steps(start, stop):
        @pl.loop(start, stop)
        def _(step):
            def mask(index):
                number = (step * (chunk // TILE_W) + index).astype(f32)
                return line_rows[...] == jnp.full((16, capacity), number, f32).astype(bf16)

            none = jnp.zeros((16, capacity), bf16)
            second, third = mask(-1), mask(-2)
            for index in range(chunk // TILE_W):
                first = mask(index)
                for part in range(TILE_W // 16):
                    rows = slice(part * 16, part * 16 + 16)
                    block = none
                    if part == 0:
                        block = jnp.where(third, wrapped[...], block)
                    block = jnp.where(second, lower[rows], block)
                    block = jnp.where(first, upper[rows], block)
                    place = pl.multiple_of(step * chunk + index * TILE_W + part * 16, 16)
                    corner_map[pl.ds(place, 16), :] = block
                second, third = first, second
            copy_in(step).wait()
            rows = rows_of(step)
            projected = dot(value_weight_ref[...], features[rows], (0, 1)).astype(bf16)
            mixed[...] += dot(projected, corner_map[rows], (1, 0))

    sample_steps(0, steps // 2)
    packed[...] = jnp.concatenate(
        [query_ref[...].astype(f32), grad_ref[...].astype(f32)], axis=0
    ).astype(bf16)
    await_all()
    keep = pltpu.make_async_copy(packed, every.at[me], local_sem)
    keep.start()
    gathers = []
    for offset in range(1, owners):
        _, device = page_peer(offset)
        gathers.append(remote(packed, every.at[me], gather_sems, offset, device))

    sample_steps(steps // 2, steps)

    keep.wait()
    for copy in gathers:
        copy.wait()
    everything = every[...].astype(f32)
    queries = everything[:, :local_queries].reshape(all_queries, width).astype(bf16)
    out_grad = everything[:, local_queries:].reshape(all_queries, width).astype(bf16)

    def head_sum(values):
        same = lax.div(
            lax.broadcasted_iota(jnp.int32, (att_width, att_width), 0), per_head
        ) == lax.div(lax.broadcasted_iota(jnp.int32, (att_width, att_width), 1), per_head)
        return lax.dot_general(
            values,
            jnp.where(same, 1.0, 0.0).astype(f32),
            (((1,), (0,)), ((), ())),
            precision=lax.Precision.HIGHEST,
            preferred_element_type=f32,
        )

    exponent = jnp.exp(dot(queries, attn_weight_ref[...], (1, 0)))
    attention = exponent / head_sum(exponent)
    attn_rows = dot(attention.astype(bf16), query_onehot[...], (0, 0))
    attn_lane = lax.broadcasted_iota(jnp.int32, (att_width, capacity), 0)
    picked = jnp.sum(jnp.where(attn_lane == column, attn_rows, zero), axis=0, keepdims=True)
    alive = lax.broadcasted_iota(jnp.int32, (1, capacity), 1) < count_ref[0, 0]
    weight = jnp.where(alive, picked, zero)
    sample_grad = dot(out_weight_ref[...], out_grad, (1, 1)).astype(bf16)
    grad_rows[...] = dot(sample_grad, query_onehot[...], (1, 0))
    dots = jnp.zeros((1, capacity), f32)
    for index in range(HEADS):
        rows = slice(index * head_width, (index + 1) * head_width)
        match = head == index
        block, pulled = grad_rows[rows], mixed[rows]
        dots = dots + jnp.where(match, jnp.sum(block * pulled, axis=0, keepdims=True), zero)
        scaled = jnp.where(match, weight, zero)
        contribution[:, rows] = (block * scaled).astype(bf16).T
        mixed[rows] = pulled * scaled
    dots = jnp.where(alive, dots, zero)
    table = jnp.where(attn_lane == column, dots, zero)
    high = table.astype(bf16)
    low = (table - high.astype(f32)).astype(bf16)
    attn_grad = dot(query_onehot[...], high, (1, 1)) + dot(query_onehot[...], low, (1, 1))
    logit = attention * (attn_grad - head_sum(attention * attn_grad))
    logit_parts[...] = logit.reshape(logit_parts.shape)
    logit_copies = []
    for offset in range(1, owners):
        peer, device = page_peer(offset)
        logit_copies.append(
            remote(logit_parts.at[peer], from_logit.at[offset], logit_sems, offset, device)
        )
    sampled = dot(mixed[...].astype(bf16), query_onehot[...], (1, 1))
    sampled_high = sampled.astype(bf16)
    sampled_low = (sampled - sampled_high.astype(f32)).astype(bf16)
    out_term = dot(sampled_high, out_grad, (1, 0)) + dot(sampled_low, out_grad, (1, 0))
    attn_term = dot(queries, logit.astype(bf16), (0, 0))
    kind = early.dtype
    per_owner = early.shape[:2]
    early[:, :, :width] = out_term.reshape(per_owner + (width,)).astype(kind)
    early[:, :, width:] = attn_term.reshape(per_owner + (att_width,)).astype(kind)
    early_sum = Exchange(
        early, early_page, early_dp, early_total, early_page_sems, early_dp_sems, early_all_sems
    )
    late_sum = Exchange(
        late, late_page, late_dp, late_total, late_page_sems, late_dp_sems, late_all_sems
    )
    early_sum.send_page()
    value_total[...] = jnp.zeros_like(value_total)

    def value_steps(first, last):
        @pl.loop(first, last)
        def _(step):
            rows = rows_of(step)
            value_rounded = dot(corner_map[rows], contribution[...], (1, 0)).astype(bf16)
            value_total[...] += dot(features[rows], value_rounded, (0, 0))
            value_grad[rows] = value_rounded
            copy_out(step).start()

    value_steps(0, steps // 2)
    early_sum.send_dp()
    value_steps(steps // 2, steps)
    late[...] = value_total[...].reshape(late.shape).astype(kind)
    late_sum.send_page()
    early_sum.send_all()
    total = logit_parts[me]
    for offset in range(1, owners):
        logit_copies[offset - 1].wait()
        total = total + from_logit[offset]
    query_grad_ref[...] = dot(total.astype(bf16), attn_weight_ref[...], (1, 1)).astype(bf16)
    late_sum.send_dp()
    early_sum.finish()
    late_sum.send_all()
    grad_scale = float(lax.axis_size("dp") * all_queries) ** (-0.5)
    total = early_total[...].astype(f32) * grad_scale
    out_weight_grad[...] = total[:, :, :width].reshape(width, width)
    attn_weight_grad[...] = total[:, :, width:].reshape(width, att_width)

    @pl.loop(0, steps)
    def _(index):
        copy_out(index).wait()

    late_sum.finish()
    total = late_total[...].astype(f32) * grad_scale
    value_weight_grad[...] = total.reshape(width, width)


def local(
    features,
    queries,
    out_grad,
    value_weight,
    attn_weight,
    out_weight,
    slot_point,
    slot_rows,
    slot_bilinear,
    slot_count,
):
    owners = lax.axis_size(PAGE)
    page_count = lax.axis_size("dp")
    local_queries = queries.shape[1]
    all_queries = local_queries * owners
    tokens, width = features.shape[1:]
    att_width = attn_weight.shape[1]
    capacity = slot_point.shape[1]
    f32, bf16 = jnp.float32, jnp.bfloat16
    vmem = pl.BlockSpec(memory_space=pltpu.VMEM)
    dma = pltpu.SemaphoreType.DMA

    any_space = pl.BlockSpec(memory_space=pl.ANY)
    rows = width // owners
    kind = bf16 if rows % 16 == 0 else f32
    early_width = width + att_width
    steps = tokens // CHUNK
    value_grad, query_grad, late, out_grads, attn_grads = pl.pallas_call(
        page_kernel,
        out_shape=(
            jax.ShapeDtypeStruct((tokens, width), bf16),
            jax.ShapeDtypeStruct((local_queries, width), bf16),
            jax.ShapeDtypeStruct((width, width), f32),
            jax.ShapeDtypeStruct((width, width), f32),
            jax.ShapeDtypeStruct((width, att_width), f32),
        ),
        in_specs=[pl.BlockSpec(memory_space=pltpu.SMEM), any_space] + [vmem] * 8,
        out_specs=(any_space, vmem, vmem, vmem, vmem),
        scratch_shapes=[
            pltpu.VMEM((owners, rows, early_width), kind),
            pltpu.VMEM((owners, rows, width), kind),
            pltpu.VMEM((16, capacity), bf16),
            pltpu.VMEM((tokens, width), bf16),
            pltpu.VMEM((tokens, width), bf16),
            pltpu.VMEM((2 * local_queries, width), bf16),
            pltpu.VMEM((owners, 2 * local_queries, width), bf16),
            pltpu.VMEM((TILE_W, capacity), bf16),
            pltpu.VMEM((TILE_W, capacity), bf16),
            pltpu.VMEM((16, capacity), bf16),
            pltpu.VMEM((tokens, capacity), bf16),
            pltpu.VMEM((width, capacity), f32),
            pltpu.VMEM((width, capacity), f32),
            pltpu.VMEM((capacity, width), bf16),
            pltpu.VMEM((all_queries, capacity), bf16),
            pltpu.VMEM((width, width), f32),
            pltpu.VMEM((owners, rows, early_width), kind),
            pltpu.VMEM((owners, rows, early_width), kind),
            pltpu.VMEM((page_count, rows, early_width), kind),
            pltpu.VMEM((owners, rows, width), kind),
            pltpu.VMEM((owners, rows, width), kind),
            pltpu.VMEM((page_count, rows, width), kind),
            pltpu.VMEM((owners, local_queries, att_width), f32),
            pltpu.VMEM((owners, local_queries, att_width), f32),
            dma,
            dma((steps,)),
            dma((steps,)),
            dma((2, owners)),
            dma((2, owners)),
            dma((2, owners)),
            dma((2, page_count)),
            dma((2, owners)),
            dma((2, owners)),
            dma((2, page_count)),
            dma((2, owners)),
        ],
        compiler_params=pltpu.CompilerParams(
            collective_id=0, has_side_effects=True, vmem_limit_bytes=60 * 1024 * 1024
        ),
    )(
        slot_count,
        features[0],
        queries[0],
        out_grad[0],
        value_weight,
        attn_weight,
        out_weight,
        slot_point,
        slot_rows[0],
        slot_bilinear[0],
    )
    feature_grad = dot(value_grad, value_weight, (1, 1)).astype(bf16)
    return feature_grad[None], query_grad[None], late, attn_grads, out_grads


def solution(mesh):
    in_specs = (
        P("dp", ("tile", "query"), None),
        P("dp", ("tile", "query"), None),
        P("dp", ("tile", "query"), None),
        P(),
        P(),
        P(),
        P("dp", ("tile", "query")),
        P("dp", None, ("tile", "query")),
        P("dp", None, ("tile", "query")),
        P("dp", ("tile", "query")),
    )
    out_specs = (P("dp", ("tile", "query"), None), P("dp", ("tile", "query"), None), P(), P(), P())
    return jax.shard_map(local, mesh=mesh, in_specs=in_specs, out_specs=out_specs, check_vma=False)
```

```python
import functools

import jax
import jax.numpy as jnp
from jax import lax
from jax.experimental import pallas as pl
from jax.experimental.pallas import tpu as pltpu
from jax.sharding import PartitionSpec as P

HEADS = 8
TILE_W = 64
MESH = pl.DeviceIdType.MESH
PAGE = ("tile", "query")
CHUNK = 1024


def dot(left, right, contract):
    return lax.dot_general(
        left, right, ((contract[:1], contract[1:]), ((), ())), preferred_element_type=jnp.float32
    )


def page_peer(offset):
    count = lax.axis_size(PAGE)
    cores = lax.axis_size("query")
    me = lax.axis_index("tile") * cores + lax.axis_index("query")
    peer = lax.rem(me + offset, count)
    return peer, {"tile": peer // cores, "query": lax.rem(peer, cores)}


def dp_peer(offset):
    return {"dp": lax.rem(lax.axis_index("dp") + offset, lax.axis_size("dp"))}


def greet_all():
    barrier = pltpu.get_barrier_semaphore()
    count = lax.axis_size(PAGE)
    pages = lax.axis_size("dp")
    for offset in range(1, count):
        pl.semaphore_signal(barrier, inc=1, device_id=page_peer(offset)[1], device_id_type=MESH)
    for offset in range(1, pages):
        pl.semaphore_signal(barrier, inc=1, device_id=dp_peer(offset), device_id_type=MESH)


def await_all():
    barrier = pltpu.get_barrier_semaphore()
    pl.semaphore_wait(barrier, lax.axis_size(PAGE) + lax.axis_size("dp") - 2)


def remote(source, target, sems, offset, device):
    copy = pltpu.make_async_remote_copy(
        src_ref=source,
        dst_ref=target,
        send_sem=sems.at[0, offset],
        recv_sem=sems.at[1, offset],
        device_id=device,
        device_id_type=MESH,
    )
    copy.start()
    return copy


class Exchange:
    def __init__(self, mine, from_page, from_dp, total, page_sems, dp_sems, all_sems):
        self.mine, self.from_page, self.from_dp, self.total = mine, from_page, from_dp, total
        self.page_sems, self.dp_sems, self.all_sems = page_sems, dp_sems, all_sems
        self.count, self.pages = lax.axis_size(PAGE), lax.axis_size("dp")

    def send_page(self):
        self.copies = []
        for offset in range(1, self.count):
            peer, device = page_peer(offset)
            target = self.from_page.at[offset]
            self.copies.append(
                remote(self.mine.at[peer], target, self.page_sems, offset, device)
            )

    def send_dp(self):
        me, _ = page_peer(0)
        total = self.mine[me].astype(jnp.float32)
        for offset in range(1, self.count):
            self.copies[offset - 1].wait()
            total = total + self.from_page[offset].astype(jnp.float32)
        self.from_dp[0] = total.astype(self.from_dp.dtype)
        self.copies = []
        for offset in range(1, self.pages):
            target = self.from_dp.at[offset]
            self.copies.append(
                remote(self.from_dp.at[0], target, self.dp_sems, offset, dp_peer(offset))
            )

    def send_all(self):
        me, _ = page_peer(0)
        for copy in self.copies:
            copy.wait()
        mine = lax.axis_index("dp")
        total = jnp.zeros(self.mine.shape[1:], jnp.float32)
        for page in range(self.pages):
            source = lax.rem(mine + self.pages - page, self.pages)
            total = total + self.from_dp[source].astype(jnp.float32)
        self.total[me] = total.astype(self.total.dtype)
        self.copies = []
        for offset in range(1, self.count):
            _, device = page_peer(offset)
            self.copies.append(
                remote(self.total.at[me], self.total.at[me], self.all_sems, offset, device)
            )

    def finish(self):
        for copy in self.copies:
            copy.wait()


def page_kernel(
    count_ref,
    features_hbm,
    query_ref,
    grad_ref,
    value_weight_ref,
    attn_weight_ref,
    out_weight_ref,
    point_ref,
    rows_ref,
    bilinear_ref,
    value_grad_hbm,
    query_grad_ref,
    early_total,
    late_total,
    line_rows,
    features,
    value_grad,
    packed,
    every,
    upper,
    lower,
    wrapped,
    corner_map,
    mixed,
    grad_rows,
    contribution,
    query_onehot,
    value_total,
    early,
    early_page,
    early_dp,
    late,
    late_page,
    late_dp,
    logit_parts,
    from_logit,
    local_sem,
    in_sems,
    out_sems,
    gather_sems,
    logit_sems,
    early_page_sems,
    early_dp_sems,
    early_all_sems,
    late_page_sems,
    late_dp_sems,
    late_all_sems,
):
    f32, bf16 = jnp.float32, jnp.bfloat16
    owners = lax.axis_size(PAGE)
    me, _ = page_peer(0)
    width = value_weight_ref.shape[0]
    att_width = attn_weight_ref.shape[1]
    per_head = att_width // HEADS
    head_width = width // HEADS
    capacity = point_ref.shape[1]
    local_queries = query_ref.shape[0]
    all_queries = local_queries * owners
    tokens = features.shape[0]
    chunk = CHUNK
    steps = tokens // chunk
    zero = jnp.zeros((), f32)

    def rows_of(index):
        return pl.ds(pl.multiple_of(index * chunk, chunk), chunk)

    def copy_in(index):
        rows = rows_of(index)
        return pltpu.make_async_copy(features_hbm.at[rows], features.at[rows], in_sems.at[index])

    def copy_out(index):
        rows = rows_of(index)
        return pltpu.make_async_copy(
            value_grad.at[rows], value_grad_hbm.at[rows], out_sems.at[index]
        )

    @pl.loop(0, steps)
    def _(index):
        copy_in(index).start()

    greet_all()
    points = point_ref[...]
    column = lax.rem(points, att_width)
    head = lax.div(column, per_head)
    base = rows_ref[0:1, :]
    x = lax.rem(base, TILE_W)
    lane = lax.broadcasted_iota(jnp.int32, (TILE_W, capacity), 0)
    here, beside = lane == x, lane == x + 1
    over = jnp.logical_and(x == TILE_W - 1, lane == 0)
    b0, b1 = bilinear_ref[0:1, :], bilinear_ref[1:2, :]
    b2, b3 = bilinear_ref[2:3, :], bilinear_ref[3:4, :]
    upper[...] = (jnp.where(here, b0, zero) + jnp.where(beside, b1, zero)).astype(bf16)
    lower[...] = (
        jnp.where(here, b2, zero) + jnp.where(beside, b3, zero) + jnp.where(over, b1, zero)
    ).astype(bf16)
    wrapped[...] = jnp.where(over, b3, zero)[0:16].astype(bf16)
    which = lax.broadcasted_iota(jnp.int32, (all_queries, capacity), 0)
    query_onehot[...] = jnp.where(which == lax.div(points, att_width), 1.0, 0.0).astype(bf16)
    mixed[...] = jnp.zeros_like(mixed)
    line = lax.div(base, TILE_W)

    line_rows[...] = jnp.broadcast_to(line.astype(f32), (16, capacity)).astype(bf16)

    def sample_steps(start, stop):
        @pl.loop(start, stop)
        def _(step):
            def mask(index):
                number = (step * (chunk // TILE_W) + index).astype(f32)
                return line_rows[...] == jnp.full((16, capacity), number, f32).astype(bf16)

            none = jnp.zeros((16, capacity), bf16)
            second, third = mask(-1), mask(-2)
            for index in range(chunk // TILE_W):
                first = mask(index)
                for part in range(TILE_W // 16):
                    rows = slice(part * 16, part * 16 + 16)
                    block = none
                    if part == 0:
                        block = jnp.where(third, wrapped[...], block)
                    block = jnp.where(second, lower[rows], block)
                    block = jnp.where(first, upper[rows], block)
                    place = pl.multiple_of(step * chunk + index * TILE_W + part * 16, 16)
                    corner_map[pl.ds(place, 16), :] = block
                second, third = first, second
            copy_in(step).wait()
            rows = rows_of(step)
            projected = dot(value_weight_ref[...], features[rows], (0, 1)).astype(bf16)
            mixed[...] += dot(projected, corner_map[rows], (1, 0))

    sample_steps(0, steps // 2)
    packed[...] = jnp.concatenate(
        [query_ref[...].astype(f32), grad_ref[...].astype(f32)], axis=0
    ).astype(bf16)
    await_all()
    keep = pltpu.make_async_copy(packed, every.at[me], local_sem)
    keep.start()
    gathers = []
    for offset in range(1, owners):
        _, device = page_peer(offset)
        gathers.append(remote(packed, every.at[me], gather_sems, offset, device))

    sample_steps(steps // 2, steps)

    keep.wait()
    for copy in gathers:
        copy.wait()
    everything = every[...].astype(f32)
    queries = everything[:, :local_queries].reshape(all_queries, width).astype(bf16)
    out_grad = everything[:, local_queries:].reshape(all_queries, width).astype(bf16)

    def head_sum(values):
        same = lax.div(
            lax.broadcasted_iota(jnp.int32, (att_width, att_width), 0), per_head
        ) == lax.div(lax.broadcasted_iota(jnp.int32, (att_width, att_width), 1), per_head)
        return lax.dot_general(
            values,
            jnp.where(same, 1.0, 0.0).astype(f32),
            (((1,), (0,)), ((), ())),
            precision=lax.Precision.HIGHEST,
            preferred_element_type=f32,
        )

    exponent = jnp.exp(dot(queries, attn_weight_ref[...], (1, 0)))
    attention = exponent / head_sum(exponent)
    attn_rows = dot(attention.astype(bf16), query_onehot[...], (0, 0))
    attn_lane = lax.broadcasted_iota(jnp.int32, (att_width, capacity), 0)
    picked = jnp.sum(jnp.where(attn_lane == column, attn_rows, zero), axis=0, keepdims=True)
    alive = lax.broadcasted_iota(jnp.int32, (1, capacity), 1) < count_ref[0, 0]
    weight = jnp.where(alive, picked, zero)
    sample_grad = dot(out_weight_ref[...], out_grad, (1, 1)).astype(bf16)
    grad_rows[...] = dot(sample_grad, query_onehot[...], (1, 0))
    dots = jnp.zeros((1, capacity), f32)
    for index in range(HEADS):
        rows = slice(index * head_width, (index + 1) * head_width)
        match = head == index
        block, pulled = grad_rows[rows], mixed[rows]
        dots = dots + jnp.where(match, jnp.sum(block * pulled, axis=0, keepdims=True), zero)
        scaled = jnp.where(match, weight, zero)
        contribution[:, rows] = (block * scaled).astype(bf16).T
        mixed[rows] = pulled * scaled
    dots = jnp.where(alive, dots, zero)
    table = jnp.where(attn_lane == column, dots, zero)
    high = table.astype(bf16)
    low = (table - high.astype(f32)).astype(bf16)
    attn_grad = dot(query_onehot[...], high, (1, 1)) + dot(query_onehot[...], low, (1, 1))
    logit = attention * (attn_grad - head_sum(attention * attn_grad))
    logit_parts[...] = logit.reshape(logit_parts.shape)
    logit_copies = []
    for offset in range(1, owners):
        peer, device = page_peer(offset)
        logit_copies.append(
            remote(logit_parts.at[peer], from_logit.at[offset], logit_sems, offset, device)
        )
    sampled = dot(mixed[...].astype(bf16), query_onehot[...], (1, 1))
    sampled_high = sampled.astype(bf16)
    sampled_low = (sampled - sampled_high.astype(f32)).astype(bf16)
    out_term = dot(sampled_high, out_grad, (1, 0)) + dot(sampled_low, out_grad, (1, 0))
    attn_term = dot(queries, logit.astype(bf16), (0, 0))
    kind = early.dtype
    per_owner = early.shape[:2]
    early[:, :, :width] = out_term.reshape(per_owner + (width,)).astype(kind)
    early[:, :, width:] = attn_term.reshape(per_owner + (att_width,)).astype(kind)
    early_sum = Exchange(
        early, early_page, early_dp, early_total, early_page_sems, early_dp_sems, early_all_sems
    )
    late_sum = Exchange(
        late, late_page, late_dp, late_total, late_page_sems, late_dp_sems, late_all_sems
    )
    early_sum.send_page()
    value_total[...] = jnp.zeros_like(value_total)

    def value_steps(first, last):
        @pl.loop(first, last)
        def _(step):
            rows = rows_of(step)
            value_rounded = dot(corner_map[rows], contribution[...], (1, 0)).astype(bf16)
            value_total[...] += dot(features[rows], value_rounded, (0, 0))
            value_grad[rows] = value_rounded
            copy_out(step).start()

    value_steps(0, steps // 2)
    early_sum.send_dp()
    value_steps(steps // 2, steps)
    late[...] = value_total[...].reshape(late.shape).astype(kind)
    late_sum.send_page()
    early_sum.send_all()
    total = logit_parts[me]
    for offset in range(1, owners):
        logit_copies[offset - 1].wait()
        total = total + from_logit[offset]
    query_grad_ref[...] = dot(total.astype(bf16), attn_weight_ref[...], (1, 1)).astype(bf16)
    late_sum.send_dp()
    early_sum.finish()
    late_sum.send_all()

    @pl.loop(0, steps)
    def _(index):
        copy_out(index).wait()

    late_sum.finish()


def last_kernel(
    grad_scale,
    value_grad_ref,
    value_weight_ref,
    query_ref,
    early_ref,
    late_ref,
    feature_grad_ref,
    query_grad_ref,
    value_weight_grad,
    attn_weight_grad,
    out_weight_grad,
):
    feature_grad_ref[...] = dot(value_grad_ref[...], value_weight_ref[...], (1, 1)).astype(
        jnp.bfloat16
    )

    @pl.when(pl.program_id(0) == 0)
    def _():
        width = value_weight_ref.shape[0]
        query_grad_ref[...] = query_ref[...]
        value_weight_grad[...] = late_ref[...].astype(jnp.float32) * grad_scale
        early = early_ref[...].astype(jnp.float32) * grad_scale
        out_weight_grad[...] = early[:, :width]
        attn_weight_grad[...] = early[:, width:]


def whole(shape):
    return pl.BlockSpec(shape, lambda step: (0,) * len(shape))


def local(
    features,
    queries,
    out_grad,
    value_weight,
    attn_weight,
    out_weight,
    slot_point,
    slot_rows,
    slot_bilinear,
    slot_count,
):
    owners = lax.axis_size(PAGE)
    page_count = lax.axis_size("dp")
    local_queries = queries.shape[1]
    all_queries = local_queries * owners
    tokens, width = features.shape[1:]
    att_width = attn_weight.shape[1]
    capacity = slot_point.shape[1]
    f32, bf16 = jnp.float32, jnp.bfloat16
    vmem = pl.BlockSpec(memory_space=pltpu.VMEM)
    dma = pltpu.SemaphoreType.DMA

    any_space = pl.BlockSpec(memory_space=pl.ANY)
    rows = width // owners
    kind = bf16 if rows % 16 == 0 else f32
    early_width = width + att_width
    steps = tokens // CHUNK
    value_grad, query_grad, early, late = pl.pallas_call(
        page_kernel,
        out_shape=(
            jax.ShapeDtypeStruct((tokens, width), bf16),
            jax.ShapeDtypeStruct((local_queries, width), bf16),
            jax.ShapeDtypeStruct((owners, rows, early_width), kind),
            jax.ShapeDtypeStruct((owners, rows, width), kind),
        ),
        in_specs=[pl.BlockSpec(memory_space=pltpu.SMEM), any_space] + [vmem] * 8,
        out_specs=(any_space, vmem, vmem, vmem),
        scratch_shapes=[
            pltpu.VMEM((16, capacity), bf16),
            pltpu.VMEM((tokens, width), bf16),
            pltpu.VMEM((tokens, width), bf16),
            pltpu.VMEM((2 * local_queries, width), bf16),
            pltpu.VMEM((owners, 2 * local_queries, width), bf16),
            pltpu.VMEM((TILE_W, capacity), bf16),
            pltpu.VMEM((TILE_W, capacity), bf16),
            pltpu.VMEM((16, capacity), bf16),
            pltpu.VMEM((tokens, capacity), bf16),
            pltpu.VMEM((width, capacity), f32),
            pltpu.VMEM((width, capacity), f32),
            pltpu.VMEM((capacity, width), bf16),
            pltpu.VMEM((all_queries, capacity), bf16),
            pltpu.VMEM((width, width), f32),
            pltpu.VMEM((owners, rows, early_width), kind),
            pltpu.VMEM((owners, rows, early_width), kind),
            pltpu.VMEM((page_count, rows, early_width), kind),
            pltpu.VMEM((owners, rows, width), kind),
            pltpu.VMEM((owners, rows, width), kind),
            pltpu.VMEM((page_count, rows, width), kind),
            pltpu.VMEM((owners, local_queries, att_width), f32),
            pltpu.VMEM((owners, local_queries, att_width), f32),
            dma,
            dma((steps,)),
            dma((steps,)),
            dma((2, owners)),
            dma((2, owners)),
            dma((2, owners)),
            dma((2, page_count)),
            dma((2, owners)),
            dma((2, owners)),
            dma((2, page_count)),
            dma((2, owners)),
        ],
        compiler_params=pltpu.CompilerParams(
            collective_id=0, has_side_effects=True, vmem_limit_bytes=60 * 1024 * 1024
        ),
    )(
        slot_count,
        features[0],
        queries[0],
        out_grad[0],
        value_weight,
        attn_weight,
        out_weight,
        slot_point,
        slot_rows[0],
        slot_bilinear[0],
    )
    grad_scale = float(page_count * all_queries) ** (-0.5)
    block = pl.BlockSpec((CHUNK, width), lambda step: (step, 0))
    feature_grad, query_grad, value_grads, attn_grads, out_grads = pl.pallas_call(
        functools.partial(last_kernel, grad_scale),
        grid=(steps,),
        out_shape=(
            jax.ShapeDtypeStruct((tokens, width), bf16),
            jax.ShapeDtypeStruct((local_queries, width), bf16),
            jax.ShapeDtypeStruct((width, width), f32),
            jax.ShapeDtypeStruct((width, att_width), f32),
            jax.ShapeDtypeStruct((width, width), f32),
        ),
        in_specs=[
            block,
            whole((width, width)),
            whole((local_queries, width)),
            whole((width, early_width)),
            whole((width, width)),
        ],
        out_specs=(
            block,
            whole((local_queries, width)),
            whole((width, width)),
            whole((width, att_width)),
            whole((width, width)),
        ),
        compiler_params=pltpu.CompilerParams(vmem_limit_bytes=60 * 1024 * 1024),
    )(
        value_grad,
        value_weight,
        query_grad,
        early.reshape(width, early_width),
        late.reshape(width, width),
    )
    return feature_grad[None], query_grad[None], value_grads, attn_grads, out_grads


def solution(mesh):
    in_specs = (
        P("dp", ("tile", "query"), None),
        P("dp", ("tile", "query"), None),
        P("dp", ("tile", "query"), None),
        P(),
        P(),
        P(),
        P("dp", ("tile", "query")),
        P("dp", None, ("tile", "query")),
        P("dp", None, ("tile", "query")),
        P("dp", ("tile", "query")),
    )
    out_specs = (P("dp", ("tile", "query"), None), P("dp", ("tile", "query"), None), P(), P(), P())
    return jax.shard_map(local, mesh=mesh, in_specs=in_specs, out_specs=out_specs, check_vma=False)
```
